32 devices in a mesh: prow: 8 (over z, y), pcol: 4 (over x, core).
Axes of the slice: x: 2, y: 2, z: 4, core: 2. Of those that a mesh axis runs over, the one named last changes fastest.
Arguments:
- ainv: float32 [20480, 20480], P('prow', 'pcol'), may hold values from -0.15625 to 0.15625
- panels: float32 [3, 20480, 512], P(None, ('prow', 'pcol')), may hold values from -0.8 to 0.8
- ancestors: int32 [3, 2560], P(None, ('prow', 'pcol')), may hold values from 0 to 1, as said below
- dinv: float32 [3, 512, 512], P(None, 'prow', 'pcol'), may hold values from -6 to 6
Outputs:
- u_panel: float32 [3, 20480, 512], P(None, ('prow', 'pcol'))
- diag: float32 [3, 512, 512], P(None, 'prow', 'pcol')
The draws below stay inside these ranges and needn't reach their ends.
Inputs may be any that keep to these rules, and one draw needn't show every extreme that they name: `ancestors`: each entry is 0 or 1; the share of ancestor blocks varies strongly between regions of the rows.
All inputs are finite; a program needn't handle non-finite values.
Results may differ from the reference program's by a relative error of at most 0.00007.
Values sent between devices are 32-bit elements; how exact they have to be, the bound alone decides.
No kernel may reach another device: no remote copies, remote signals or barrier semaphores. Data moves between devices by JAX's collectives and lax.ppermute only.
A program may use at most 192 MiB of HBM per device.

```python
import jax
import jax.numpy as jnp
from jax import lax

M = 20480
S = 512
NSUP = 3
BLK = 8
N_PROW = 8
N_PCOL = 4


def draw_ancestors(key, part):
    blocks = M // BLK
    regions = (blocks + 79) // 80
    first_key, second_key = jax.random.split(jax.random.fold_in(key, 17))
    levels = jax.random.randint(first_key, (NSUP, regions), 0, 101)
    rolls = jax.random.randint(second_key, (NSUP, blocks), 0, 100)
    region_of = jnp.arange(blocks, dtype=jnp.int32) // 80
    limits = jnp.take(levels, region_of, axis=1)
    return (rolls < limits).astype(jnp.int32)


def level_of(own_key, shape, pieces, least, largest):
    gain = 1.0
    for position, blocks in pieces:
        heights = jax.random.uniform(jax.random.fold_in(jax.random.fold_in(own_key, 6), position), (blocks,), jnp.float32, least / len(pieces), largest / len(pieces))
        gain = gain * jnp.repeat(jnp.exp(heights), shape[position] // blocks).reshape((-1,) + (1,) * (len(shape) - 1 - position))
    return gain


def centred(rng, dims, scale, reach, pieces=(), kind=jnp.bfloat16):
    drawn = scale * jax.random.normal(rng, dims, jnp.float32)
    if pieces:
        drawn = drawn * level_of(rng, dims, pieces, -0.22, 0.18)
    return jnp.clip(drawn, -reach, reach).astype(kind)


def setup_inputs(seed: int = 0) -> dict:
    seeds = jax.random.split(jax.random.key(seed), 5)
    ainv = centred(seeds[0], (M, M), (M // 16) ** -0.5, 0.15625, ((0, 8), (1, 4)), jnp.float32)
    panels = centred(seeds[1], (NSUP, M, S), 0.1, 0.8, ((1, 32),), jnp.float32)
    ancestors = draw_ancestors(jax.random.fold_in(seeds[4], 71), 0)
    dinv = centred(seeds[3], (NSUP, S, S), 1.0, 6.0, ((1, 8), (2, 4)), jnp.float32)
    return dict(ainv=ainv, panels=panels, ancestors=ancestors, dinv=dinv)


def reference(ainv, panels, ancestors, dinv):
    dev_rows = M // (N_PROW * N_PCOL)
    col_width = M // N_PCOL
    stored = jnp.arange(M, dtype=jnp.int32)
    col_owner = stored // col_width
    within = stored % col_width
    row_owner = within // dev_rows
    offset = within % dev_rows
    source = ((row_owner * N_PCOL + col_owner) * dev_rows + offset).astype(jnp.int32)
    row_flags = jnp.repeat(ancestors, BLK, axis=1).astype(jnp.float32)
    masked = panels * row_flags[:, :, None]
    reordered = jnp.take(masked, source, axis=1)

    def product_of(piece):
        return jnp.dot(ainv, piece, precision=lax.Precision.HIGHEST)

    products = lax.map(product_of, reordered)
    u_panel = -(row_flags[:, :, None] * products)
    diag = dinv - jnp.einsum("srn,srm->snm", masked, u_panel, precision=lax.Precision.HIGHEST)
    return u_panel, diag
```

```python
import functools

import jax
import jax.numpy as jnp
from jax import lax
from jax.experimental import pallas as pl
from jax.experimental.pallas import tpu as pltpu
from jax.sharding import PartitionSpec as P

LANES = 128
CHAIN = 4


def is_power_of_two(n):
    return n > 0 and n & (n - 1) == 0


def plain_on_device(ainv, panels, ancestors, dinv):
    block = panels.shape[1] // ancestors.shape[1]
    row_flags = jnp.repeat(ancestors, block, axis=1).astype(jnp.float32)
    masked = panels * row_flags[:, :, None]
    results = []
    for member in range(panels.shape[0]):
        gathered = lax.all_gather(masked[member], "prow", axis=0, tiled=True)
        summed_one = jnp.dot(ainv, gathered, precision=lax.Precision.HIGHEST)
        results.append(lax.psum_scatter(summed_one, "pcol", scatter_dimension=0, tiled=True))
    u_panel = -(row_flags[:, :, None] * jnp.stack(results, axis=0))
    local_terms = jnp.einsum("srn,srm->snm", masked, u_panel, precision=lax.Precision.HIGHEST)
    totals = lax.psum(local_terms, ("prow", "pcol"))
    row_count, col_count = dinv.shape[1:]
    own_rows = lax.dynamic_slice_in_dim(totals, lax.axis_index("prow") * row_count, row_count, 1)
    own_block = lax.dynamic_slice_in_dim(own_rows, lax.axis_index("pcol") * col_count, col_count, 2)
    return u_panel, dinv - own_block


def follow(value, earlier):
    earlier = [array for array in earlier if array is not None]
    return lax.optimization_barrier((value, *earlier))[0] if earlier else value


def split(x):
    high = x.astype(jnp.bfloat16)
    low = (x - high.astype(jnp.float32)).astype(jnp.bfloat16)
    return high, low


def product_kernel(piece_counts, has_sum, n_out, *refs):
    n_items = len(piece_counts)
    refs = refs[1:]
    a_refs, refs = refs[:n_items], refs[n_items:]
    n_pieces = sum(piece_counts)
    piece_refs, refs = refs[:n_pieces], refs[n_pieces:]
    if has_sum:
        sum_ref, refs = refs[0], refs[1:]
    out_refs, (token_ref, high_ref, low_ref) = refs[:n_out], refs[n_out:]

    @pl.when(pl.program_id(0) == 0)
    def _():
        row = 0
        for piece in piece_refs:
            rows = piece.shape[0]
            high_ref[row : row + rows, :], low_ref[row : row + rows, :] = split(piece[...])
            row += rows
        token_ref[...] = jnp.zeros_like(token_ref)

    halves = [split(a_ref[...]) for a_ref in a_refs]
    a_high = jnp.concatenate([high for high, _ in halves], axis=1)
    a_low = jnp.concatenate([low for _, low in halves], axis=1)
    times = functools.partial(jnp.dot, preferred_element_type=jnp.float32)
    total = times(a_high, high_ref[...]) + (times(a_low, high_ref[...]) + times(a_high, low_ref[...]))
    if has_sum:
        total = sum_ref[...] + total
    if n_out == 1:
        out_refs[0][...] = total
    else:
        away = pl.program_id(0) < pl.num_programs(0) // 2

        @pl.when(away)
        def _():
            out_refs[1][...] = total

        @pl.when(jnp.logical_not(away))
        def _():
            out_refs[0][...] = total


def add_products(ainv, column, items, regions, running, tile, parted=False, after=()):
    depth = sum(piece.shape[0] for piece in items[0])
    width = items[0][0].shape[1]
    blocks = ainv.shape[0] // depth
    per = depth // tile
    steps = blocks * per
    n_items = len(items)
    prefetch = follow(jnp.stack([column, *regions]).astype(jnp.int32), after)

    def row_of(i):
        if not parted:
            return i
        away = i < steps // 2
        j = jnp.where(away, i, i - steps // 2)
        return (2 * (j // per) + jnp.where(away, 1, 0)) * per + j % per

    def a_row(i, s):
        row = row_of(i)
        return ((row // per) ^ s[0]) * per + row % per

    once = pl.Buffered(buffer_count=1)
    in_specs = [
        pl.BlockSpec((tile, depth), functools.partial(lambda k, i, s: (a_row(i, s), s[k]), k + 1))
        for k in range(n_items)
    ]
    pieces = [piece for item in items for piece in item]
    in_specs += [pl.BlockSpec(piece.shape, lambda i, s: (0, 0), pipeline_mode=once) for piece in pieces]
    operands = [ainv] * n_items + pieces
    aliases = {}
    if running is not None:
        if not parted:
            aliases = {len(operands) + 1: 0}
        in_specs.append(pl.BlockSpec((tile, width), lambda i, s: (row_of(i), 0)))
        operands.append(running)
    rows = blocks * depth
    if parted:
        out_shape = [jax.ShapeDtypeStruct((rows // 2, width), jnp.float32)] * 2
        out_specs = [
            pl.BlockSpec((tile, width), lambda i, s: (jnp.maximum(i - steps // 2, 0), 0)),
            pl.BlockSpec((tile, width), lambda i, s: (jnp.minimum(i, steps // 2 - 1), 0)),
        ]
    else:
        out_shape = [jax.ShapeDtypeStruct((rows, width), jnp.float32)]
        out_specs = [pl.BlockSpec((tile, width), lambda i, s: (i, 0))]
    n_out = len(out_shape)
    out_shape.append(jax.ShapeDtypeStruct((8, LANES), jnp.float32))
    out_specs.append(pl.BlockSpec((8, LANES), lambda i, s: (0, 0)))
    outs = pl.pallas_call(
        functools.partial(product_kernel, tuple(len(item) for item in items), running is not None, n_out),
        out_shape=out_shape,
        grid_spec=pltpu.PrefetchScalarGridSpec(
            num_scalar_prefetch=1,
            grid=(steps,),
            in_specs=in_specs,
            out_specs=out_specs,
            scratch_shapes=[pltpu.VMEM((n_items * depth, width), jnp.bfloat16)] * 2,
        ),
        input_output_aliases=aliases,
        cost_estimate=pl.CostEstimate(flops=1, bytes_accessed=1, transcendentals=0),
        compiler_params=pltpu.CompilerParams(vmem_limit_bytes=52 * 1024 * 1024),
    )(prefetch, *operands)
    return tuple(outs)


def chain_order(length):
    orders = [[place] for place in range(length)]
    span = 1
    while span < length:
        grown = []
        for place in range(length):
            block = place // span
            edge = (block + 1) * span if block % 2 == 0 else block * span - 1
            grown.append(orders[place] + orders[edge][:span])
        orders = grown
        span *= 2
    return orders


def chain_hops(length, span):
    hops = [[] for _ in range(span)]
    for start in range(0, length, 2 * span):
        for hop in range(span):
            below, above = start + span - 1 - hop, start + span + hop
            if hop == 0:
                hops[0] += [(below, above), (above, below)]
            else:
                hops[hop] += [(below + 1, below), (above - 1, above)]
    return hops


def column_groups(sups, wide):
    last = wide // 2
    each = (sups * wide - last) // 2
    groups, at = [], 0
    for size in (each, each, last):
        pieces, end = [], at + size
        while at < end:
            member, start = at // wide, at % wide
            width = min(wide - start, end - at)
            pieces.append((member, start, width))
            at += width
        groups.append(pieces)
    return groups


def fast_on_device(n_prow, n_pcol, ainv, panels, ancestors, dinv):
    sups, depth, wide = panels.shape
    length = n_prow // 2
    half = depth // 2
    own_p = lax.axis_index("prow")
    own_c = lax.axis_index("pcol")
    place, side = own_p // 2, own_p % 2
    flags = jnp.repeat(ancestors, depth // ancestors.shape[1], axis=1).astype(jnp.float32)
    cols, rows_own = dinv.shape[2], dinv.shape[1]

    side_pairs = [(p, p ^ 1) for p in range(n_prow)]

    def chain_pairs(pairs):
        return [(2 * a + y, 2 * b + y) for a, b in pairs for y in (0, 1)]

    def prow_pairs(bit):
        return [(p, p ^ bit) for p in range(n_prow)]

    def pcol_pairs(bit):
        return [(c, c ^ bit) for c in range(n_pcol)]

    prow_bits = [1 << k for k in range(n_prow.bit_length() - 1)]
    pcol_bits = [1 << k for k in range(n_pcol.bit_length() - 1)]

    orders = chain_order(length)
    own_order = [jnp.take(jnp.array(column, jnp.int32), place) for column in zip(*orders)]
    same_side = [2 * z + side for z in own_order]
    other_side = [2 * z + 1 - side for z in own_order]

    masked = [panels[member] * flags[member][:, None] for member in range(sups)]
    due = {}

    def want(tick, *arrays):
        due.setdefault(tick, []).extend(arrays)

    class Group:
        def __init__(self, pieces):
            self.pieces = pieces
            self.here = [jnp.concatenate([masked[m][:, at : at + width] for m, at, width in pieces], axis=1)]
            self.there = []
            self.running = None

    first_group, second_group, last_group = [Group(pieces) for pieces in column_groups(sups, wide)]

    def moves(group, step, after):
        hops1 = chain_pairs(chain_hops(length, 1)[0])
        send = lambda value, pairs: lax.ppermute(follow(value, after), "prow", pairs)
        here, there = group.here, group.there
        new = []
        if step == 0:
            there.append([send(here[0], side_pairs)])
            new.append(there[0][0])
            group.first = send(here[0], hops1)
            new.append(group.first)
            if length >= 4:
                hops2 = chain_hops(length, 2)
                group.over = send(here[0], chain_pairs(hops2[0]))
                new.append(group.over)
            here.append(group.first)
        elif step == 1:
            there.append([send(here[1][:half], side_pairs)])
            new.append(there[1][0])
            if length >= 4:
                hops2 = chain_hops(length, 2)
                inward = send(group.over, chain_pairs(hops2[1]))
                group.over2 = send(here[1], chain_pairs(hops2[0]))
                new += [inward, group.over2]
                here.append(jnp.where(at_edge, group.over, inward))
        elif step == 2:
            inward = send(group.over2, chain_pairs(chain_hops(length, 2)[1]))
            there.append([send(here[2], side_pairs)])
            new += [inward, there[2][0]]
            here.append(jnp.where(at_edge, group.over2, inward))
        elif step == 3:
            second = send(there[0][0][half:], hops1)
            there[1].append(second)
            there.append([send(here[3], side_pairs)])
            new += [second, there[3][0]]
        return new

    at_edge = jnp.logical_or(place == length // 2 - 1, place == length // 2)

    def items(group, step):
        here, there = group.here, group.there
        wanted = [((0, 0), (1, 0)), ((0, 1), (0, 2)), ((0, 3), (1, 2)), ((1, 3), (1, 1))][step]
        return [(there[k], other_side[k]) if over else ([here[k]], same_side[k]) for over, k in wanted]

    def sum_rows(kept, away, tick):
        for index, bit in enumerate(pcol_bits):
            if tick + 1 + index < len(arrived):
                away = follow(away, arrived[tick + 1 + index])
            received = lax.ppermute(away, "pcol", pcol_pairs(bit))
            total = kept + received
            if total.shape[0] == depth:
                want(tick + 5, received)
                return total
            blocks = total.reshape(total.shape[0] // (2 * depth), 2, depth, total.shape[1])
            kept = blocks[:, 0].reshape(-1, total.shape[1])
            away = blocks[:, 1].reshape(-1, total.shape[1])
            want(tick + 2 if tick + 2 < len(ticks) else tick + 1, away)

    def sum_diagonal(terms, start, tick):
        width = terms.shape[2]
        count = width // cols
        low_bits = [bit for bit in pcol_bits if bit < count]
        blocks = {
            q: lax.dynamic_slice_in_dim(terms, ((own_c ^ q) % count) * cols, cols, 2) for q in range(count)
        }
        for bit in low_bits:
            away = [q for q in sorted(blocks) if q & bit]
            moved = lax.ppermute(jnp.stack([blocks[q] for q in away]), "pcol", pcol_pairs(bit))
            want(tick, moved)
            tick += 1
            blocks = {q ^ bit: blocks[q ^ bit] + moved[k] for k, q in enumerate(away)}
        value = blocks[0].reshape(terms.shape[0], n_prow, rows_own, cols)
        for bit in prow_bits:
            paired = value.reshape(value.shape[0], value.shape[1] // 2, 2, rows_own, cols)
            mine = (own_p // bit) % 2
            keep = lax.dynamic_index_in_dim(paired, mine, 2, keepdims=False)
            send = lax.dynamic_index_in_dim(paired, 1 - mine, 2, keepdims=False)
            value = keep + lax.ppermute(send, "prow", prow_pairs(bit))
            want(tick, value)
            tick += 1
        value = value[:, 0]
        for bit in pcol_bits:
            if bit not in low_bits:
                value = value + lax.ppermute(value, "pcol", pcol_pairs(bit))
        return value

    def transposed_product(left, right):
        return lax.dot_general(
            left, right, (((0,), (0,)), ((), ())), precision=lax.Precision.HIGH,
            preferred_element_type=jnp.float32,
        )

    near = [masked[-1]]
    for index, bit in enumerate(pcol_bits):
        moved = [lax.ppermute(value, "pcol", pcol_pairs(bit)) for value in near]
        want(1 + 2 * index, *moved)
        near += moved
    near_kept = jnp.concatenate(near[0::2], axis=0)
    near_away = jnp.concatenate(near[1::2], axis=0)

    ticks = [(group, step) for step in range(4) for group in (first_group, second_group)]
    ticks += [(last_group, step) for step in range(4)]
    turns = 8
    arrived, tokens = [], []
    parts = [[] for _ in range(sups)]
    diag = [[] for _ in range(sups)]

    def start(k):
        group, step = ticks[k]
        lead = 2 if k <= turns else 1
        after = (arrived[k - lead] if k >= lead else []) + ([tokens[k - lead - 1]] if k > lead else [])
        arrived.append(moves(group, step, after))

    started = 0
    for k, (group, step) in enumerate(ticks):
        while started < len(ticks) and started <= (k + 2 if k + 2 <= turns else max(k + 1, turns)):
            start(started)
            started += 1
        if k == len(ticks) - 1:
            products = [
                transposed_product(masked[m], follow(jnp.concatenate(parts[m], axis=1), tokens[-1:]))
                for m in range(sups - 1)
            ]
            for m, value in enumerate(sum_diagonal(jnp.stack(products), 0, k + 1)):
                diag[m].append(value)
        chosen = items(group, step)
        last = step == 3
        *sums, token = add_products(
            ainv, own_c, [c[0] for c in chosen], [c[1] for c in chosen], group.running, depth,
            parted=last, after=arrived[k] + (tokens[-1:]) + due.get(k, []),
        )
        tokens.append(token)
        if not last:
            group.running = sums[0]
            continue
        kept, away = sums
        if group is last_group:
            diag[-1].append(-(transposed_product(near_kept, kept) + transposed_product(near_away, away)))
        summed = sum_rows(kept, away, k)
        at = 0
        for member, _, width in group.pieces:
            part = -(flags[member][:, None] * summed[:, at : at + width])
            at += width
            parts[member].append(part)
            if member == sups - 1 and group is not last_group:
                diag[-1].append(transposed_product(masked[member], follow(part, tokens[-1:])))
    u_panel = jnp.stack([jnp.concatenate(part, axis=1) for part in parts])
    diag[-1] = [sum_diagonal(jnp.concatenate(diag[-1], axis=1)[None], 0, len(ticks))[0]]
    return u_panel, dinv - jnp.stack([found[0] for found in diag])


def solution(mesh):
    n_prow, n_pcol = mesh.shape["prow"], mesh.shape["pcol"]

    def on_device(ainv, panels, ancestors, dinv):
        depth, wide = panels.shape[1:]
        fits = (
            is_power_of_two(n_prow)
            and is_power_of_two(n_pcol)
            and n_prow == 2 * CHAIN
            and (2 * panels.shape[0] - 1) * wide % (4 * LANES) == 0
            and panels.shape[0] >= 2
            and n_pcol >= 2
            and depth % LANES == 0
            and wide % (2 * LANES) == 0
            and wide % n_prow == 0
            and ainv.shape == (depth * n_pcol, depth * n_prow)
        )
        if fits:
            return fast_on_device(n_prow, n_pcol, ainv, panels, ancestors, dinv)
        return plain_on_device(ainv, panels, ancestors, dinv)

    in_specs = (
        P("prow", "pcol"),
        P(None, ("prow", "pcol"), None),
        P(None, ("prow", "pcol")),
        P(None, "prow", "pcol"),
    )
    out_specs = (P(None, ("prow", "pcol"), None), P(None, "prow", "pcol"))
    return jax.shard_map(on_device, mesh=mesh, in_specs=in_specs, out_specs=out_specs, check_vma=False)
```

```python
import functools

import jax
import jax.numpy as jnp
from jax import lax
from jax.experimental import pallas as pl
from jax.experimental.pallas import tpu as pltpu
from jax.sharding import PartitionSpec as P

LANES = 128
CHAIN = 4


def is_power_of_two(n):
    return n > 0 and n & (n - 1) == 0


def plain_on_device(ainv, panels, ancestors, dinv):
    block = panels.shape[1] // ancestors.shape[1]
    row_flags = jnp.repeat(ancestors, block, axis=1).astype(jnp.float32)
    masked = panels * row_flags[:, :, None]
    results = []
    for member in range(panels.shape[0]):
        gathered = lax.all_gather(masked[member], "prow", axis=0, tiled=True)
        summed_one = jnp.dot(ainv, gathered, precision=lax.Precision.HIGHEST)
        results.append(lax.psum_scatter(summed_one, "pcol", scatter_dimension=0, tiled=True))
    u_panel = -(row_flags[:, :, None] * jnp.stack(results, axis=0))
    local_terms = jnp.einsum("srn,srm->snm", masked, u_panel, precision=lax.Precision.HIGHEST)
    totals = lax.psum(local_terms, ("prow", "pcol"))
    row_count, col_count = dinv.shape[1:]
    own_rows = lax.dynamic_slice_in_dim(totals, lax.axis_index("prow") * row_count, row_count, 1)
    own_block = lax.dynamic_slice_in_dim(own_rows, lax.axis_index("pcol") * col_count, col_count, 2)
    return u_panel, dinv - own_block


def follow(value, earlier):
    earlier = [array for array in earlier if array is not None]
    return lax.optimization_barrier((value, *earlier))[0] if earlier else value


def split(x):
    high = x.astype(jnp.bfloat16)
    low = (x - high.astype(jnp.float32)).astype(jnp.bfloat16)
    return high, low


def product_kernel(piece_counts, has_sum, n_out, *refs):
    n_items = len(piece_counts)
    refs = refs[1:]
    a_refs, refs = refs[:n_items], refs[n_items:]
    n_pieces = sum(piece_counts)
    piece_refs, refs = refs[:n_pieces], refs[n_pieces:]
    if has_sum:
        sum_ref, refs = refs[0], refs[1:]
    out_refs, (token_ref, high_ref, low_ref) = refs[:n_out], refs[n_out:]

    @pl.when(pl.program_id(0) == 0)
    def _():
        row = 0
        for piece in piece_refs:
            rows = piece.shape[0]
            high_ref[row : row + rows, :], low_ref[row : row + rows, :] = split(piece[...])
            row += rows
        token_ref[...] = jnp.zeros_like(token_ref)

    halves = [split(a_ref[...]) for a_ref in a_refs]
    a_high = jnp.concatenate([high for high, _ in halves], axis=1)
    a_low = jnp.concatenate([low for _, low in halves], axis=1)
    times = functools.partial(jnp.dot, preferred_element_type=jnp.float32)
    total = times(a_high, high_ref[...]) + (times(a_low, high_ref[...]) + times(a_high, low_ref[...]))
    if has_sum:
        total = sum_ref[...] + total
    if n_out == 1:
        out_refs[0][...] = total
    else:
        away = pl.program_id(0) < pl.num_programs(0) // 2

        @pl.when(away)
        def _():
            out_refs[1][...] = total

        @pl.when(jnp.logical_not(away))
        def _():
            out_refs[0][...] = total


def add_products(ainv, column, items, regions, running, tile, parted=False, after=()):
    depth = sum(piece.shape[0] for piece in items[0])
    width = items[0][0].shape[1]
    blocks = ainv.shape[0] // depth
    per = depth // tile
    steps = blocks * per
    n_items = len(items)
    prefetch = follow(jnp.stack([column, *regions]).astype(jnp.int32), after)

    def row_of(i):
        if not parted:
            return i
        away = i < steps // 2
        j = jnp.where(away, i, i - steps // 2)
        return (2 * (j // per) + jnp.where(away, 1, 0)) * per + j % per

    def a_row(i, s):
        row = row_of(i)
        return ((row // per) ^ s[0]) * per + row % per

    once = pl.Buffered(buffer_count=1)
    in_specs = [
        pl.BlockSpec((tile, depth), functools.partial(lambda k, i, s: (a_row(i, s), s[k]), k + 1))
        for k in range(n_items)
    ]
    pieces = [piece for item in items for piece in item]
    in_specs += [pl.BlockSpec(piece.shape, lambda i, s: (0, 0), pipeline_mode=once) for piece in pieces]
    operands = [ainv] * n_items + pieces
    aliases = {}
    if running is not None:
        if not parted:
            aliases = {len(operands) + 1: 0}
        in_specs.append(pl.BlockSpec((tile, width), lambda i, s: (row_of(i), 0)))
        operands.append(running)
    rows = blocks * depth
    if parted:
        out_shape = [jax.ShapeDtypeStruct((rows // 2, width), jnp.float32)] * 2
        out_specs = [
            pl.BlockSpec((tile, width), lambda i, s: (jnp.maximum(i - steps // 2, 0), 0)),
            pl.BlockSpec((tile, width), lambda i, s: (jnp.minimum(i, steps // 2 - 1), 0)),
        ]
    else:
        out_shape = [jax.ShapeDtypeStruct((rows, width), jnp.float32)]
        out_specs = [pl.BlockSpec((tile, width), lambda i, s: (i, 0))]
    n_out = len(out_shape)
    out_shape.append(jax.ShapeDtypeStruct((8, LANES), jnp.float32))
    out_specs.append(pl.BlockSpec((8, LANES), lambda i, s: (0, 0)))
    outs = pl.pallas_call(
        functools.partial(product_kernel, tuple(len(item) for item in items), running is not None, n_out),
        out_shape=out_shape,
        grid_spec=pltpu.PrefetchScalarGridSpec(
            num_scalar_prefetch=1,
            grid=(steps,),
            in_specs=in_specs,
            out_specs=out_specs,
            scratch_shapes=[pltpu.VMEM((n_items * depth, width), jnp.bfloat16)] * 2,
        ),
        input_output_aliases=aliases,
        cost_estimate=pl.CostEstimate(flops=1, bytes_accessed=1, transcendentals=0),
        compiler_params=pltpu.CompilerParams(vmem_limit_bytes=52 * 1024 * 1024),
    )(prefetch, *operands)
    return tuple(outs)


def chain_order(length):
    orders = [[place] for place in range(length)]
    span = 1
    while span < length:
        grown = []
        for place in range(length):
            block = place // span
            edge = (block + 1) * span if block % 2 == 0 else block * span - 1
            grown.append(orders[place] + orders[edge][:span])
        orders = grown
        span *= 2
    return orders


def chain_hops(length, span):
    hops = [[] for _ in range(span)]
    for start in range(0, length, 2 * span):
        for hop in range(span):
            below, above = start + span - 1 - hop, start + span + hop
            if hop == 0:
                hops[0] += [(below, above), (above, below)]
            else:
                hops[hop] += [(below + 1, below), (above - 1, above)]
    return hops


def column_groups(sups, wide):
    last = wide // 2
    each = (sups * wide - last) // 2
    groups, at = [], 0
    for size in (each, each, last):
        pieces, end = [], at + size
        while at < end:
            member, start = at // wide, at % wide
            width = min(wide - start, end - at)
            pieces.append((member, start, width))
            at += width
        groups.append(pieces)
    return groups


def fast_on_device(n_prow, n_pcol, ainv, panels, ancestors, dinv):
    sups, depth, wide = panels.shape
    length = n_prow // 2
    own_p = lax.axis_index("prow")
    own_c = lax.axis_index("pcol")
    place, side = own_p // 2, own_p % 2
    flags = jnp.repeat(ancestors, depth // ancestors.shape[1], axis=1).astype(jnp.float32)
    cols, rows_own = dinv.shape[2], dinv.shape[1]

    side_pairs = [(p, p ^ 1) for p in range(n_prow)]

    def chain_pairs(pairs):
        return [(2 * a + y, 2 * b + y) for a, b in pairs for y in (0, 1)]

    def prow_pairs(bit):
        return [(p, p ^ bit) for p in range(n_prow)]

    def pcol_pairs(bit):
        return [(c, c ^ bit) for c in range(n_pcol)]

    prow_bits = [1 << k for k in range(n_prow.bit_length() - 1)]
    pcol_bits = [1 << k for k in range(n_pcol.bit_length() - 1)]

    orders = chain_order(length)
    own_order = [jnp.take(jnp.array(column, jnp.int32), place) for column in zip(*orders)]
    same_side = [2 * z + side for z in own_order]
    other_side = [2 * z + 1 - side for z in own_order]

    masked = [panels[member] * flags[member][:, None] for member in range(sups)]
    due = {}

    def want(tick, *arrays):
        due.setdefault(tick, []).extend(arrays)

    class Group:
        def __init__(self, pieces):
            self.pieces = pieces
            self.here = [jnp.concatenate([masked[m][:, at : at + width] for m, at, width in pieces], axis=1)]
            self.there = []
            self.running = None

    first_group, second_group, last_group = [Group(pieces) for pieces in column_groups(sups, wide)]

    def moves(group, step, after):
        hops1 = chain_pairs(chain_hops(length, 1)[0])
        send = lambda value, pairs: lax.ppermute(follow(value, after), "prow", pairs)
        here, there = group.here, group.there
        new = []
        if step == 0:
            there.append([send(here[0], side_pairs)])
            new.append(there[0][0])
            group.first = send(here[0], hops1)
            new.append(group.first)
            if length >= 4:
                hops2 = chain_hops(length, 2)
                group.over = send(here[0], chain_pairs(hops2[0]))
                new.append(group.over)
            here.append(group.first)
        elif step == 1:
            there.append([send(here[1], side_pairs)])
            new.append(there[1][0])
            if length >= 4:
                hops2 = chain_hops(length, 2)
                inward = send(group.over, chain_pairs(hops2[1]))
                group.over2 = send(here[1], chain_pairs(hops2[0]))
                new += [inward, group.over2]
                here.append(jnp.where(at_edge, group.over, inward))
        elif step == 2:
            inward = send(group.over2, chain_pairs(chain_hops(length, 2)[1]))
            there.append([send(here[2], side_pairs)])
            new += [inward, there[2][0]]
            here.append(jnp.where(at_edge, group.over2, inward))
        elif step == 3:
            there.append([send(here[3], side_pairs)])
            new.append(there[3][0])
        return new

    at_edge = jnp.logical_or(place == length // 2 - 1, place == length // 2)

    def items(group, step):
        here, there = group.here, group.there
        if group is last_group:
            plan = [((0, 0), (1, 0)), ((0, 1), (0, 2), (1, 1)), (), ((0, 3), (1, 2), (1, 3))]
        else:
            plan = [((0, 0), (1, 0)), ((0, 1), (0, 2)), ((0, 3), (1, 1)), ((1, 3), (1, 2))]
        wanted = plan[step]
        return [(there[k], other_side[k]) if over else ([here[k]], same_side[k]) for over, k in wanted]

    def sum_rows(group, kept, away, tick):
        for bit in pcol_bits:
            if bit == 1 and group is second_group:
                away = follow(away, arrived[tick + 1])
            if group is last_group and bit == pcol_bits[-1]:
                away = follow(away, row_sums[-1:])
            received = lax.ppermute(away, "pcol", pcol_pairs(bit))
            if kept.shape[0] == depth:
                if group is first_group:
                    want(tick + 4, received)
                row_sums.append(received)
                return kept, received, away
            total = kept + received
            blocks = total.reshape(total.shape[0] // (2 * depth), 2, depth, total.shape[1])
            kept = blocks[:, 0].reshape(-1, total.shape[1])
            away = blocks[:, 1].reshape(-1, total.shape[1])
            want(tick + 2, away)

    def sum_diagonal(terms, first_bits):
        blocks = {q: lax.dynamic_slice_in_dim(terms, (own_c ^ q) * cols, cols, 2) for q in range(n_pcol)}

        def halve_columns(blocks, bit):
            away = [q for q in sorted(blocks) if q & bit]
            moved = lax.ppermute(jnp.stack([blocks[q] for q in away]), "pcol", pcol_pairs(bit))
            return {q ^ bit: blocks[q ^ bit] + moved[k] for k, q in enumerate(away)}

        for bit in first_bits:
            blocks = halve_columns(blocks, bit)
            sent.append(blocks[0])
        order = sorted(blocks)
        value = jnp.stack([blocks[q] for q in order]).reshape(len(order) * terms.shape[0], n_prow, rows_own, cols)
        for bit in prow_bits:
            paired = value.reshape(value.shape[0], value.shape[1] // 2, 2, rows_own, cols)
            mine = (own_p // bit) % 2
            keep = lax.dynamic_index_in_dim(paired, mine, 2, keepdims=False)
            send = lax.dynamic_index_in_dim(paired, 1 - mine, 2, keepdims=False)
            value = keep + lax.ppermute(send, "prow", prow_pairs(bit))
            sent.append(value)
        value = value.reshape(len(order), terms.shape[0], rows_own, cols)
        blocks = {q: value[k] for k, q in enumerate(order)}
        for bit in pcol_bits:
            if bit not in first_bits:
                blocks = halve_columns(blocks, bit)
        return blocks[0]

    def transposed_product(left, right):
        return lax.dot_general(
            left, right, (((0,), (0,)), ((), ())), precision=lax.Precision.HIGH,
            preferred_element_type=jnp.float32,
        )

    row_sums = []
    near = [masked[-1]]

    def exchange_near(bit, tick):
        after = arrived[tick - 1]
        moved = [lax.ppermute(follow(value, after), "pcol", pcol_pairs(bit)) for value in near]
        want(tick + 2, *moved)
        near.extend(moved)

    ticks = [(group, step) for step in range(4) for group in (first_group, second_group)]
    ticks += [(last_group, step) for step in range(4)]
    turns = 8
    arrived, tokens = [], []
    parts = [[] for _ in range(sups)]
    last_terms = []

    def start(k):
        group, step = ticks[k]
        if k <= turns:
            after = arrived[k - 2] + [tokens[k - 2]] if k >= 2 else []
        else:
            after = arrived[k - 1] + [tokens[k - 2]]
        arrived.append(moves(group, step, after))

    start(0)
    start(1)
    for k, (group, step) in enumerate(ticks):
        if 1 <= k <= len(pcol_bits):
            exchange_near(pcol_bits[k - 1], k)
        chosen = items(group, step)
        if not chosen:
            want(k + 1, *due.get(k, []))
            start(k + 1)
            continue
        last = step == 3
        *sums, token = add_products(
            ainv, own_c, [c[0] for c in chosen], [c[1] for c in chosen], group.running, depth,
            parted=last, after=arrived[k] + tokens[-1:] + due.get(k, []),
        )
        tokens.append(token)
        if k + 2 <= turns:
            start(k + 2)
        elif k + 2 < len(ticks) - 1:
            start(k + 2)
        if not last:
            group.running = sums[0]
            continue
        kept, away = sums
        if group is last_group:
            near_kept = jnp.concatenate(near[0::2], axis=0)
            near_away = jnp.concatenate(near[1::2], axis=0)
            last_terms.append(-(transposed_product(near_kept, kept) + transposed_product(near_away, away)))
        own_sum, other_sum, last_sent = sum_rows(group, kept, away, k)
        if group is last_group:
            sent = [last_sent]
            last_diag = sum_diagonal(jnp.concatenate(last_terms, axis=1)[None], pcol_bits[:1])
            others_after = sent[:2]
            other_sum = follow(other_sum, sent[2:3])
        summed = own_sum + other_sum
        at = 0
        for member, _, width in group.pieces:
            part = -(flags[member][:, None] * summed[:, at : at + width])
            at += width
            parts[member].append(part)
            if member == sups - 1 and group is not last_group:
                last_terms.append(transposed_product(masked[member], follow(part, tokens[-1:])))
    u_whole = [jnp.concatenate(part, axis=1) for part in parts]
    terms = [transposed_product(masked[m], follow(u_whole[m], others_after)) for m in range(sups - 1)]
    other_diag = sum_diagonal(jnp.stack(terms), pcol_bits[:1])
    return jnp.stack(u_whole), dinv - jnp.concatenate([other_diag, last_diag], axis=0)


def solution(mesh):
    n_prow, n_pcol = mesh.shape["prow"], mesh.shape["pcol"]

    def on_device(ainv, panels, ancestors, dinv):
        depth, wide = panels.shape[1:]
        fits = (
            is_power_of_two(n_prow)
            and is_power_of_two(n_pcol)
            and n_prow == 2 * CHAIN
            and (2 * panels.shape[0] - 1) * wide % (4 * LANES) == 0
            and panels.shape[0] >= 2
            and n_pcol >= 2
            and depth % LANES == 0
            and wide % (2 * LANES) == 0
            and wide % n_prow == 0
            and ainv.shape == (depth * n_pcol, depth * n_prow)
        )
        if fits:
            return fast_on_device(n_prow, n_pcol, ainv, panels, ancestors, dinv)
        return plain_on_device(ainv, panels, ancestors, dinv)

    in_specs = (
        P("prow", "pcol"),
        P(None, ("prow", "pcol"), None),
        P(None, ("prow", "pcol")),
        P(None, "prow", "pcol"),
    )
    out_specs = (P(None, ("prow", "pcol"), None), P(None, "prow", "pcol"))
    return jax.shard_map(on_device, mesh=mesh, in_specs=in_specs, out_specs=out_specs, check_vma=False)
```

```python
import functools

import jax
import jax.numpy as jnp
from jax import lax
from jax.experimental import pallas as pl
from jax.experimental.pallas import tpu as pltpu
from jax.sharding import PartitionSpec as P

LANES = 128
CHAIN = 4


def is_power_of_two(n):
    return n > 0 and n & (n - 1) == 0


def plain_on_device(ainv, panels, ancestors, dinv):
    block = panels.shape[1] // ancestors.shape[1]
    row_flags = jnp.repeat(ancestors, block, axis=1).astype(jnp.float32)
    masked = panels * row_flags[:, :, None]
    results = []
    for member in range(panels.shape[0]):
        gathered = lax.all_gather(masked[member], "prow", axis=0, tiled=True)
        summed_one = jnp.dot(ainv, gathered, precision=lax.Precision.HIGHEST)
        results.append(lax.psum_scatter(summed_one, "pcol", scatter_dimension=0, tiled=True))
    u_panel = -(row_flags[:, :, None] * jnp.stack(results, axis=0))
    local_terms = jnp.einsum("srn,srm->snm", masked, u_panel, precision=lax.Precision.HIGHEST)
    totals = lax.psum(local_terms, ("prow", "pcol"))
    row_count, col_count = dinv.shape[1:]
    own_rows = lax.dynamic_slice_in_dim(totals, lax.axis_index("prow") * row_count, row_count, 1)
    own_block = lax.dynamic_slice_in_dim(own_rows, lax.axis_index("pcol") * col_count, col_count, 2)
    return u_panel, dinv - own_block


def follow(value, earlier):
    earlier = [array for array in earlier if array is not None]
    return lax.optimization_barrier((value, *earlier))[0] if earlier else value


def split(x):
    high = x.astype(jnp.bfloat16)
    low = (x - high.astype(jnp.float32)).astype(jnp.bfloat16)
    return high, low


def product_kernel(piece_counts, has_sum, n_out, *refs):
    n_items = len(piece_counts)
    refs = refs[1:]
    a_refs, refs = refs[:n_items], refs[n_items:]
    n_pieces = sum(piece_counts)
    piece_refs, refs = refs[:n_pieces], refs[n_pieces:]
    if has_sum:
        sum_ref, refs = refs[0], refs[1:]
    out_refs, (token_ref, high_ref, low_ref) = refs[:n_out], refs[n_out:]

    @pl.when(pl.program_id(0) == 0)
    def _():
        row = 0
        for piece in piece_refs:
            rows = piece.shape[0]
            high_ref[row : row + rows, :], low_ref[row : row + rows, :] = split(piece[...])
            row += rows
        token_ref[...] = jnp.zeros_like(token_ref)

    halves = [split(a_ref[...]) for a_ref in a_refs]
    a_high = jnp.concatenate([high for high, _ in halves], axis=1)
    a_low = jnp.concatenate([low for _, low in halves], axis=1)
    times = functools.partial(jnp.dot, preferred_element_type=jnp.float32)
    total = times(a_high, high_ref[...]) + (times(a_low, high_ref[...]) + times(a_high, low_ref[...]))
    if has_sum:
        total = sum_ref[...] + total
    if n_out == 1:
        out_refs[0][...] = total
    else:
        away = pl.program_id(0) < pl.num_programs(0) // 2

        @pl.when(away)
        def _():
            out_refs[1][...] = total

        @pl.when(jnp.logical_not(away))
        def _():
            out_refs[0][...] = total


def add_products(ainv, column, items, regions, running, tile, parted=False, after=()):
    depth = sum(piece.shape[0] for piece in items[0])
    width = items[0][0].shape[1]
    blocks = ainv.shape[0] // depth
    per = depth // tile
    steps = blocks * per
    n_items = len(items)
    prefetch = follow(jnp.stack([column, *regions]).astype(jnp.int32), after)

    def row_of(i):
        if not parted:
            return i
        away = i < steps // 2
        j = jnp.where(away, i, i - steps // 2)
        return (2 * (j // per) + jnp.where(away, 1, 0)) * per + j % per

    def a_row(i, s):
        row = row_of(i)
        return ((row // per) ^ s[0]) * per + row % per

    once = pl.Buffered(buffer_count=1)
    in_specs = [
        pl.BlockSpec((tile, depth), functools.partial(lambda k, i, s: (a_row(i, s), s[k]), k + 1))
        for k in range(n_items)
    ]
    pieces = [piece for item in items for piece in item]
    in_specs += [pl.BlockSpec(piece.shape, lambda i, s: (0, 0), pipeline_mode=once) for piece in pieces]
    operands = [ainv] * n_items + pieces
    aliases = {}
    if running is not None:
        if not parted:
            aliases = {len(operands) + 1: 0}
        in_specs.append(pl.BlockSpec((tile, width), lambda i, s: (row_of(i), 0)))
        operands.append(running)
    rows = blocks * depth
    if parted:
        out_shape = [jax.ShapeDtypeStruct((rows // 2, width), jnp.float32)] * 2
        out_specs = [
            pl.BlockSpec((tile, width), lambda i, s: (jnp.maximum(i - steps // 2, 0), 0)),
            pl.BlockSpec((tile, width), lambda i, s: (jnp.minimum(i, steps // 2 - 1), 0)),
        ]
    else:
        out_shape = [jax.ShapeDtypeStruct((rows, width), jnp.float32)]
        out_specs = [pl.BlockSpec((tile, width), lambda i, s: (i, 0))]
    n_out = len(out_shape)
    out_shape.append(jax.ShapeDtypeStruct((8, LANES), jnp.float32))
    out_specs.append(pl.BlockSpec((8, LANES), lambda i, s: (0, 0)))
    outs = pl.pallas_call(
        functools.partial(product_kernel, tuple(len(item) for item in items), running is not None, n_out),
        out_shape=out_shape,
        grid_spec=pltpu.PrefetchScalarGridSpec(
            num_scalar_prefetch=1,
            grid=(steps,),
            in_specs=in_specs,
            out_specs=out_specs,
            scratch_shapes=[pltpu.VMEM((n_items * depth, width), jnp.bfloat16)] * 2,
        ),
        input_output_aliases=aliases,
        cost_estimate=pl.CostEstimate(flops=1, bytes_accessed=1, transcendentals=0),
        compiler_params=pltpu.CompilerParams(vmem_limit_bytes=52 * 1024 * 1024),
    )(prefetch, *operands)
    return tuple(outs)


def chain_order(length):
    orders = [[place] for place in range(length)]
    span = 1
    while span < length:
        grown = []
        for place in range(length):
            block = place // span
            edge = (block + 1) * span if block % 2 == 0 else block * span - 1
            grown.append(orders[place] + orders[edge][:span])
        orders = grown
        span *= 2
    return orders


def chain_hops(length, span):
    hops = [[] for _ in range(span)]
    for start in range(0, length, 2 * span):
        for hop in range(span):
            below, above = start + span - 1 - hop, start + span + hop
            if hop == 0:
                hops[0] += [(below, above), (above, below)]
            else:
                hops[hop] += [(below + 1, below), (above - 1, above)]
    return hops


def column_groups(sups, wide):
    last = wide // 2
    each = (sups * wide - last) // 2
    groups, at = [], 0
    for size in (each, each, last):
        pieces, end = [], at + size
        while at < end:
            member, start = at // wide, at % wide
            width = min(wide - start, end - at)
            pieces.append((member, start, width))
            at += width
        groups.append(pieces)
    return groups


def fast_on_device(n_prow, n_pcol, ainv, panels, ancestors, dinv):
    sups, depth, wide = panels.shape
    length = n_prow // 2
    own_p = lax.axis_index("prow")
    own_c = lax.axis_index("pcol")
    place, side = own_p // 2, own_p % 2
    flags = jnp.repeat(ancestors, depth // ancestors.shape[1], axis=1).astype(jnp.float32)
    cols, rows_own = dinv.shape[2], dinv.shape[1]

    side_pairs = [(p, p ^ 1) for p in range(n_prow)]

    def chain_pairs(pairs):
        return [(2 * a + y, 2 * b + y) for a, b in pairs for y in (0, 1)]

    def prow_pairs(bit):
        return [(p, p ^ bit) for p in range(n_prow)]

    def pcol_pairs(bit):
        return [(c, c ^ bit) for c in range(n_pcol)]

    prow_bits = [1 << k for k in range(n_prow.bit_length() - 1)]
    pcol_bits = [1 << k for k in range(n_pcol.bit_length() - 1)]

    orders = chain_order(length)
    own_order = [jnp.take(jnp.array(column, jnp.int32), place) for column in zip(*orders)]
    same_side = [2 * z + side for z in own_order]
    other_side = [2 * z + 1 - side for z in own_order]

    masked = [panels[member] * flags[member][:, None] for member in range(sups)]
    due = {}

    def want(tick, *arrays):
        due.setdefault(tick, []).extend(arrays)

    class Group:
        def __init__(self, pieces):
            self.pieces = pieces
            self.here = [jnp.concatenate([masked[m][:, at : at + width] for m, at, width in pieces], axis=1)]
            self.there = []
            self.running = None

    first_group, second_group, last_group = [Group(pieces) for pieces in column_groups(sups, wide)]

    def moves(group, step, after):
        hops1 = chain_pairs(chain_hops(length, 1)[0])
        send = lambda value, pairs: lax.ppermute(follow(value, after), "prow", pairs)
        here, there = group.here, group.there
        new = []
        if step == 0:
            there.append([send(here[0], side_pairs)])
            new.append(there[0][0])
            group.first = send(here[0], hops1)
            new.append(group.first)
            if length >= 4:
                hops2 = chain_hops(length, 2)
                group.over = send(here[0], chain_pairs(hops2[0]))
                new.append(group.over)
            here.append(group.first)
        elif step == 1:
            there.append([send(here[1], side_pairs)])
            new.append(there[1][0])
            if length >= 4:
                hops2 = chain_hops(length, 2)
                inward = send(group.over, chain_pairs(hops2[1]))
                group.over2 = send(here[1], chain_pairs(hops2[0]))
                new += [inward, group.over2]
                here.append(jnp.where(at_edge, group.over, inward))
        elif step == 2:
            inward = send(group.over2, chain_pairs(chain_hops(length, 2)[1]))
            there.append([send(here[2], side_pairs)])
            new += [inward, there[2][0]]
            here.append(jnp.where(at_edge, group.over2, inward))
        elif step == 3:
            there.append([send(here[3], side_pairs)])
            new.append(there[3][0])
        return new

    at_edge = jnp.logical_or(place == length // 2 - 1, place == length // 2)

    def items(group, step):
        here, there = group.here, group.there
        if group is last_group:
            plan = [((0, 0), (1, 0)), ((0, 1), (0, 2), (1, 1)), (), ((0, 3), (1, 2), (1, 3))]
        else:
            plan = [((0, 0), (1, 0)), ((0, 1), (0, 2)), ((0, 3), (1, 1)), ((1, 3), (1, 2))]
        wanted = plan[step]
        return [(there[k], other_side[k]) if over else ([here[k]], same_side[k]) for over, k in wanted]

    def sum_rows(group, kept, away, tick):
        for bit in pcol_bits:
            if bit == 1 and group is second_group:
                away = follow(away, arrived[tick + 1])
            if group is last_group and bit == pcol_bits[-1]:
                away = follow(away, row_sums[-1:])
            received = lax.ppermute(away, "pcol", pcol_pairs(bit))
            if kept.shape[0] == depth:
                if group is first_group:
                    want(tick + 4, received)
                row_sums.append(received)
                return kept, received, away
            total = kept + received
            blocks = total.reshape(total.shape[0] // (2 * depth), 2, depth, total.shape[1])
            kept = blocks[:, 0].reshape(-1, total.shape[1])
            away = blocks[:, 1].reshape(-1, total.shape[1])
            want(tick + 2, away)

    def sum_diagonal(terms, first_bits):
        blocks = {q: lax.dynamic_slice_in_dim(terms, (own_c ^ q) * cols, cols, 2) for q in range(n_pcol)}

        def halve_columns(blocks, bit):
            away = [q for q in sorted(blocks) if q & bit]
            moved = lax.ppermute(jnp.stack([blocks[q] for q in away]), "pcol", pcol_pairs(bit))
            return {q ^ bit: blocks[q ^ bit] + moved[k] for k, q in enumerate(away)}

        for bit in first_bits:
            blocks = halve_columns(blocks, bit)
            sent.append(blocks[0])
        order = sorted(blocks)
        value = jnp.stack([blocks[q] for q in order]).reshape(len(order) * terms.shape[0], n_prow, rows_own, cols)
        for bit in prow_bits:
            paired = value.reshape(value.shape[0], value.shape[1] // 2, 2, rows_own, cols)
            mine = (own_p // bit) % 2
            keep = lax.dynamic_index_in_dim(paired, mine, 2, keepdims=False)
            send = lax.dynamic_index_in_dim(paired, 1 - mine, 2, keepdims=False)
            value = keep + lax.ppermute(send, "prow", prow_pairs(bit))
            sent.append(value)
        value = value.reshape(len(order), terms.shape[0], rows_own, cols)
        blocks = {q: value[k] for k, q in enumerate(order)}
        for bit in pcol_bits:
            if bit not in first_bits:
                blocks = halve_columns(blocks, bit)
        return blocks[0]

    def transposed_product(left, right):
        return lax.dot_general(
            left, right, (((0,), (0,)), ((), ())), precision=lax.Precision.HIGH,
            preferred_element_type=jnp.float32,
        )

    row_sums = []
    near = [masked[-1]]

    def exchange_near(bit, tick):
        after = arrived[tick - 1]
        moved = [lax.ppermute(follow(value, after), "pcol", pcol_pairs(bit)) for value in near]
        want(tick + 2, *moved)
        near.extend(moved)

    ticks = [(group, step) for step in range(4) for group in (first_group, second_group)]
    ticks += [(last_group, step) for step in range(4)]
    turns = 8
    arrived, tokens = [], []
    parts = [[] for _ in range(sups)]
    last_terms = []

    def start(k):
        group, step = ticks[k]
        if k <= turns:
            after = arrived[k - 2] + [tokens[k - 2]] if k >= 2 else []
        else:
            after = arrived[k - 1] + [tokens[k - 2]]
        arrived.append(moves(group, step, after))

    start(0)
    start(1)
    for k, (group, step) in enumerate(ticks):
        if 1 <= k <= len(pcol_bits):
            exchange_near(pcol_bits[k - 1], k)
        chosen = items(group, step)
        if not chosen:
            want(k + 1, *due.get(k, []))
            start(k + 1)
            continue
        last = step == 3
        if k == len(ticks) - 1:
            first_terms = transposed_product(masked[0], follow(jnp.concatenate(parts[0], axis=1), tokens[-1:]))
            want(k, first_terms)
        *sums, token = add_products(
            ainv, own_c, [c[0] for c in chosen], [c[1] for c in chosen], group.running, depth,
            parted=last, after=arrived[k] + tokens[-1:] + due.get(k, []),
        )
        tokens.append(token)
        if k + 2 <= turns:
            start(k + 2)
        elif k + 2 < len(ticks) - 1:
            start(k + 2)
        if not last:
            group.running = sums[0]
            continue
        kept, away = sums
        if group is last_group:
            near_kept = jnp.concatenate(near[0::2], axis=0)
            near_away = jnp.concatenate(near[1::2], axis=0)
            last_terms.append(-(transposed_product(near_kept, kept) + transposed_product(near_away, away)))
        own_sum, other_sum, last_sent = sum_rows(group, kept, away, k)
        if group is last_group:
            sent = [last_sent]
            last_diag = sum_diagonal(jnp.concatenate(last_terms, axis=1)[None], pcol_bits[:1])
            others_after = sent[:2]
            other_sum = follow(other_sum, sent[2:3])
        summed = own_sum + other_sum
        at = 0
        for member, _, width in group.pieces:
            part = -(flags[member][:, None] * summed[:, at : at + width])
            at += width
            parts[member].append(part)
            if member == sups - 1 and group is not last_group:
                last_terms.append(transposed_product(masked[member], follow(part, tokens[-1:])))
    u_whole = [jnp.concatenate(part, axis=1) for part in parts]
    terms = [transposed_product(masked[m], follow(u_whole[m], others_after)) for m in range(1, sups - 1)]
    terms = [first_terms] + terms
    other_diag = sum_diagonal(jnp.stack(terms), pcol_bits[:1])
    return jnp.stack(u_whole), dinv - jnp.concatenate([other_diag, last_diag], axis=0)


def solution(mesh):
    n_prow, n_pcol = mesh.shape["prow"], mesh.shape["pcol"]

    def on_device(ainv, panels, ancestors, dinv):
        depth, wide = panels.shape[1:]
        fits = (
            is_power_of_two(n_prow)
            and is_power_of_two(n_pcol)
            and n_prow == 2 * CHAIN
            and (2 * panels.shape[0] - 1) * wide % (4 * LANES) == 0
            and panels.shape[0] >= 2
            and n_pcol >= 2
            and depth % LANES == 0
            and wide % (2 * LANES) == 0
            and wide % n_prow == 0
            and ainv.shape == (depth * n_pcol, depth * n_prow)
        )
        if fits:
            return fast_on_device(n_prow, n_pcol, ainv, panels, ancestors, dinv)
        return plain_on_device(ainv, panels, ancestors, dinv)

    in_specs = (
        P("prow", "pcol"),
        P(None, ("prow", "pcol"), None),
        P(None, ("prow", "pcol")),
        P(None, "prow", "pcol"),
    )
    out_specs = (P(None, ("prow", "pcol"), None), P(None, "prow", "pcol"))
    return jax.shard_map(on_device, mesh=mesh, in_specs=in_specs, out_specs=out_specs, check_vma=False)
```
